32 devices in a mesh: rows: 8 (over z, x), feat: 4 (over y, core).
Axes of the slice: x: 2, y: 2, z: 4, core: 2. Of those that a mesh axis runs over, the one named last changes fastest.
Arguments:
- scores: float32 [262144, 64], P(('rows', 'feat'))
- labels: int32 [262144], P('rows'), may hold values from 0 to 63
- bins: int32 [256, 262144], P('feat', 'rows'), may hold values from 0 to 63
- elected: int32 [64, 16], P(None, 'feat'), may hold values from 0 to 255, as said below
Outputs:
- gains: float32 [64, 16, 63], P('rows', 'feat')
The draws below stay inside these ranges and needn't reach their ends.
Inputs may be any that keep to these rules, and one draw needn't show every extreme that they name: `elected`: for every class and every j < 4, columns j * 4 to (j + 1) * 4 - 1 hold 4 distinct features of the range j * 64 to (j + 1) * 64 - 1.
All inputs are finite; a program needn't handle non-finite values.
Results may differ from the reference program's by a relative error of at most 0.0026.
Values may be sent and summed in bfloat16 or wider, within the bound.
No kernel may reach another device: no remote copies, remote signals or barrier semaphores. Data moves between devices by JAX's collectives and lax.ppermute only.
A program may use at most 64 MiB of HBM per device.

```python
import jax
import jax.numpy as jnp
from jax import lax

C = 64
F = 256
BINS = 64
EPG = 4
ROWS = 262144
FGRP = 64
ELECT = 16


def common_bins(key):
    return jax.random.randint(jax.random.fold_in(key, 11), (F, ROWS), 0, BINS, jnp.int32)


def common_elected(key):
    group_count = F // FGRP
    keys = jax.random.split(jax.random.fold_in(key, 12), C * group_count)
    picks = jax.vmap(lambda sub_key: jax.random.permutation(sub_key, FGRP)[:EPG])(keys)
    picks = picks.reshape(C, group_count, EPG).astype(jnp.int32)
    starts = (jnp.arange(group_count, dtype=jnp.int32) * FGRP)[None, :, None]
    return (picks + starts).reshape(C, ELECT).astype(jnp.int32)


def draw_bins(key, part):
    return common_bins(key)


def draw_elected(key, part):
    return common_elected(key)


def draw_scores(key, part):
    bin_table = common_bins(key)
    chosen = common_elected(key)
    first_bins = bin_table[chosen[:, 0], :]
    last_bins = bin_table[chosen[:, ELECT - 1], :]
    ramp = (first_bins + last_bins).astype(jnp.float32).T / (2.0 * (BINS - 1))
    spread = 0.4 + 2.4 * ramp
    key_a = jax.random.fold_in(jax.random.fold_in(key, 13), 0)
    base = jax.random.normal(key_a, (ROWS, C), jnp.float32)
    return spread * base - 0.5 * spread * spread


def place_ends(drawn, own_key, low, high):
    spot = [jax.random.randint(jax.random.fold_in(own_key, axis), (), 0, length) for axis, length in enumerate(drawn.shape)]
    widest = drawn.shape.index(max(drawn.shape))
    next_to = spot[:widest] + [(spot[widest] + 1) % drawn.shape[widest]] + spot[widest + 1:]
    return drawn.at[tuple(spot)].set(low).at[tuple(next_to)].set(high)


def setup_inputs(seed: int = 0) -> dict:
    key_list = jax.random.split(jax.random.key(seed), 5)
    return {
        "scores": draw_scores(jax.random.fold_in(key_list[4], 71), 0),
        "labels": place_ends(jax.random.randint(key_list[1], (ROWS,), 0, C), jax.random.fold_in(key_list[1], 1), 0, C - 1).astype(jnp.int32),
        "bins": draw_bins(jax.random.fold_in(key_list[4], 71), 0),
        "elected": draw_elected(jax.random.fold_in(key_list[4], 71), 0),
    }


l2_penalty = 1.0


def grad_columns(scores, labels):
    row_max = jnp.max(scores, axis=1, keepdims=True)
    expon = jnp.exp(scores - row_max)
    probs = expon / jnp.sum(expon, axis=1, keepdims=True)
    target = (labels[:, None] == jnp.arange(scores.shape[1], dtype=jnp.int32)[None, :]).astype(jnp.float32)
    grad = (probs - target).astype(jnp.bfloat16)
    hess = (probs * (1.0 - probs)).astype(jnp.bfloat16)
    return grad, hess


def split_gains(hist):
    left_g = jnp.cumsum(hist[..., 0], axis=-1)
    left_h = jnp.cumsum(hist[..., 1], axis=-1)
    tot_g = left_g[..., -1:]
    tot_h = left_h[..., -1:]
    right_g = tot_g - left_g
    right_h = tot_h - left_h
    split_gain = 0.5 * (left_g * left_g / (left_h + l2_penalty) + right_g * right_g / (right_h + l2_penalty) - tot_g * tot_g / (tot_h + l2_penalty))
    return split_gain[..., :-1]


def reference(scores, labels, bins, elected):
    grad, hess = grad_columns(scores, labels)
    grad_t = grad.astype(jnp.float32).T
    hess_t = hess.astype(jnp.float32).T
    n_elect = elected.shape[1]
    n_rows = scores.shape[0]
    offsets = (jnp.arange(n_elect, dtype=jnp.int32) * BINS)[:, None]

    def per_class(packed):
        chosen, gcol, hcol = packed
        index_all = (bins[chosen, :] + offsets).reshape(-1)
        gsum = jax.ops.segment_sum(jnp.broadcast_to(gcol[None, :], (n_elect, n_rows)).reshape(-1), index_all, num_segments=n_elect * BINS)
        hsum = jax.ops.segment_sum(jnp.broadcast_to(hcol[None, :], (n_elect, n_rows)).reshape(-1), index_all, num_segments=n_elect * BINS)
        return jnp.stack([gsum.reshape(n_elect, BINS), hsum.reshape(n_elect, BINS)], axis=-1)

    hist = lax.map(per_class, (elected, grad_t, hess_t))
    return split_gains(hist)
```

```python
import jax
import jax.numpy as jnp
from jax import lax
from jax.experimental import pallas as pl
from jax.experimental.pallas import tpu as pltpu
from jax.sharding import PartitionSpec as P

BINS = 64
LANES = 128
l2_penalty = 1.0

SURE = -1e-30

F8 = jnp.float8_e4m3fn
FULL = 256.0
LOW = 16.0


def rounded(x):
    far = x * 65537.0
    return far - (far - x)


def nudged(code, side, wanted):
    code = rounded(code)
    found = rounded(code + side)
    unit = jnp.abs(code) * (1.25 / 256.0)
    return jnp.where(wanted > found, code + unit, jnp.where(wanted < found, code - unit, code))


def score_kernel(n_blocks, scores_ref, labels_ref, coded_ref, score_slots, label_slot, sems):
    rows = scores_ref.shape[1]
    block = rows // n_blocks
    begin = pl.multiple_of(lax.axis_index("feat") * rows, rows)
    label_copy = pltpu.make_async_copy(labels_ref.at[:, pl.ds(begin, rows)], label_slot, sems.at[n_blocks])
    label_copy.start()
    copies = [
        pltpu.make_async_copy(
            scores_ref.at[:, pl.ds(i * block, block)], score_slots.at[:, pl.ds(i * block, block)], sems.at[i]
        )
        for i in range(n_blocks)
    ]
    for copy in copies:
        copy.start()
    label_copy.wait()
    for i in range(n_blocks):
        copies[i].wait()
        where = pl.ds(i * block, block)
        coded_ref[:, where] = encode(score_slots[:, where], label_slot[:, where]).astype(coded_ref.dtype)


def encode(scores, labels):
    is_label = lax.broadcasted_iota(jnp.int32, scores.shape, 0) == labels
    row_max = jnp.max(scores, axis=0, keepdims=True)
    expon = jnp.exp(scores - row_max)
    probs = expon / jnp.sum(expon, axis=0, keepdims=True)
    top = jnp.max(probs, axis=0, keepdims=True)
    labelled = jnp.sum(jnp.where(is_label, probs, 0.0), axis=0, keepdims=True)
    top_code = nudged(jnp.minimum(top - 1.0, SURE), 1.0, rounded(top))
    label_code = jnp.where(
        labelled > 0.5,
        jnp.minimum(labelled - 1.0, SURE),
        nudged(labelled, -1.0, rounded(labelled - 1.0)),
    )
    return jnp.where(is_label, label_code, jnp.where(probs > 0.5, top_code, probs))


def in_hbm(array):
    return pltpu.with_memory_space_constraint(array, pltpu.HBM)


def score(scores, labels):
    classes, rows = scores.shape
    n_blocks = 4
    far = pl.BlockSpec(memory_space=pltpu.HBM)
    return pl.pallas_call(
        lambda *refs: score_kernel(n_blocks, *refs),
        in_specs=[far, far],
        out_specs=pl.BlockSpec(memory_space=pltpu.VMEM),
        scratch_shapes=[
            pltpu.VMEM((classes, rows), jnp.float32),
            pltpu.VMEM((1, rows), jnp.int32),
            pltpu.SemaphoreType.DMA((n_blocks + 1,)),
        ],
        out_shape=jax.ShapeDtypeStruct((classes, rows), jnp.bfloat16),
        compiler_params=pltpu.CompilerParams(vmem_limit_bytes=48 << 20),
        cost_estimate=pl.CostEstimate(
            flops=10 * rows * classes, bytes_accessed=6 * rows * classes, transcendentals=rows * classes
        ),
    )(in_hbm(scores), in_hbm(labels))


def decode(coded, labels, first_class):
    classes, length = coded.shape
    value = coded.astype(jnp.float32)
    is_label = lax.broadcasted_iota(jnp.int32, (classes, length), 0) + first_class == labels
    above = value < 0.0
    side = jnp.where(above, 1.0, -1.0)
    crossed = is_label != above
    near = jnp.where(crossed, rounded(value + side) - side, value)
    whole = jnp.where(crossed, side, 0.0)
    size = jnp.abs(value)
    return near, whole, near - (size - size * size)


def power_of_two(values):
    largest = jnp.max(jnp.abs(values), axis=1, keepdims=True)
    scale = jnp.ones_like(largest)
    back = jnp.ones_like(largest)
    for power in (16, 8, 4, 2, 1):
        small = largest * scale <= 0.5**power
        scale = jnp.where(small, scale * 2.0**power, scale)
        back = jnp.where(small, back * 0.5**power, back)
    return scale * FULL, back * (1.0 / FULL)


def put_columns(coded_ref, labels, first_class, count, columns_ref, backs_ref):
    classes = coded_ref.shape[0]
    near, whole, square = decode(coded_ref[pl.ds(first_class, count), :], labels, first_class)

    def put(kind, columns, back):
        where = pl.ds(kind * classes + first_class, count)
        columns_ref[where, :] = columns
        backs_ref[where, :] = jnp.broadcast_to(back, (count, backs_ref.shape[1]))

    scale, back = power_of_two(near)
    scaled = near * scale
    high = scaled.astype(F8)
    put(0, high, back)
    put(1, ((scaled - high.astype(jnp.float32)) * LOW).astype(F8), back * (1.0 / LOW))
    scale, back = power_of_two(square)
    put(2, (square * scale).astype(F8), back)
    put(3, whole.astype(F8), jnp.ones_like(back))


def back_row(backs_ref):
    rows, lanes = backs_ref.shape
    sub = lax.broadcasted_iota(jnp.int32, (lanes, lanes), 0)
    diagonal = sub == lax.broadcasted_iota(jnp.int32, (lanes, lanes), 1)
    parts = [
        jnp.sum(jnp.where(diagonal, backs_ref[start : start + lanes, :], 0.0), axis=0, keepdims=True)
        for start in range(0, rows, lanes)
    ]
    return jnp.concatenate(parts, axis=1)


def add_tile(bins_ref, columns_ref, back, sums_ref, first_feature, count, fresh):
    length = bins_ref.shape[1]
    bin_ids = lax.broadcasted_iota(jnp.int32, (BINS, length), 0).astype(jnp.int8)
    one = jnp.ones((BINS, length), F8)
    zero = jnp.zeros((BINS, length), F8)
    parts = []
    for offset in range(count):
        codes = jnp.broadcast_to(bins_ref[pl.ds(first_feature + offset, 1), :], (BINS, length))
        parts.append(jnp.where(codes.astype(jnp.int8) == bin_ids, one, zero))
    added = lax.dot_general(
        jnp.concatenate(parts, axis=0),
        columns_ref[...],
        (((1,), (1,)), ((), ())),
        preferred_element_type=jnp.float32,
    )
    added = added * back
    where = pl.ds(pl.multiple_of(first_feature * BINS, count * BINS), count * BINS)
    if fresh:
        sums_ref[where, :] = added
    else:
        sums_ref[where, :] += added


def hist_kernel(group, length, shifts, n_feat, cores, chained, *refs):
    count = len(shifts)
    elect_ref, bins_ref, labels_ref = refs[:3]
    coded_refs = refs[3 : 3 + count]
    refs = refs[3 + count :]
    if chained:
        before_ref, refs = refs[0], refs[1:]
    out_ref, sums_ref, bin_slots, label_slots, coded_slots = refs[:5]
    columns = refs[5:7]
    backs = refs[7:9]
    bin_sems, label_sems, coded_sems, elect_slot, elect_sem = refs[9:]
    classes, rows = coded_refs[0].shape
    features = bins_ref.shape[0]
    place = lax.axis_index("feat")
    halves = rows // length
    blocks = [(part, half) for part in range(count) for half in range(halves)]

    bin_copies, code_copies = [], []
    for index, (part, half) in enumerate(blocks):
        turn, swapped = shifts[part]
        source = (place - turn * cores + n_feat) % n_feat
        if swapped:
            source = source + 1 - 2 * (source % 2)
        begin = pl.multiple_of(source * rows + half * length, length)
        bin_copies.append(
            pltpu.make_async_copy(
                bins_ref.at[:, pl.ds(begin, length)], bin_slots.at[index % 2], bin_sems.at[index]
            )
        )
        code_copies.append(
            (
                pltpu.make_async_copy(
                    coded_refs[part].at[:, pl.ds(half * length, length)],
                    coded_slots.at[index],
                    coded_sems.at[index],
                ),
                pltpu.make_async_copy(
                    labels_ref.at[:, pl.ds(begin, length)], label_slots.at[index], label_sems.at[index]
                ),
            )
        )
    elect_copy = pltpu.make_async_copy(elect_ref, elect_slot, elect_sem)
    elect_copy.start()
    for copy in code_copies[0]:
        copy.start()
    bin_copies[0].start()
    bin_copies[1].start()
    for pair in code_copies[1:]:
        for copy in pair:
            copy.start()

    tiles = features // group
    turns = 2 if tiles % 2 == 0 and classes % 64 == 0 else 1
    each = classes // turns
    for copy in code_copies[0]:
        copy.wait()
    put_columns(coded_slots.at[0], label_slots[0], 0, classes, columns[0], backs[0])

    for index in range(len(blocks)):
        now, later = index % 2, (index + 1) % 2
        back = back_row(backs[now])
        bin_copies[index].wait()
        more = index + 1 < len(blocks)
        if more:
            for copy in code_copies[index + 1]:
                copy.wait()

        def one_turn(turn, carry):
            for tile in range(tiles // turns):
                feature = (turn * (tiles // turns) + tile) * group
                add_tile(bin_slots.at[now], columns[now], back, sums_ref, feature, group, index == 0)
            if more:
                first = pl.multiple_of(turn * each, each)
                put_columns(
                    coded_slots.at[index + 1], label_slots[index + 1], first, each, columns[later], backs[later]
                )
            return carry

        lax.fori_loop(0, turns, one_turn, 0)
        if index + 2 < len(blocks):
            bin_copies[index + 2].start()

    elect_copy.wait()
    elected = jnp.concatenate([elect_slot[...]] * 4, axis=1) - place * features
    elect = elected.shape[0]

    def pick(feature, picked):
        rows = sums_ref[pl.ds(pl.multiple_of(feature * BINS, BINS), BINS), :]
        return tuple(jnp.where(elected[e : e + 1, :] == feature, rows, picked[e]) for e in range(elect))

    nothing = tuple(jnp.zeros((BINS, 4 * classes), jnp.float32) for _ in range(elect))
    picked = lax.fori_loop(0, features, pick, nothing, unroll=2)
    by_class = jnp.concatenate([part.T for part in picked], axis=1)
    near = by_class[:classes] + by_class[classes : 2 * classes]
    square = by_class[2 * classes : 3 * classes]
    whole = by_class[3 * classes :]
    kinds = (near + whole, near - square)
    owners, _, owned, _ = out_ref.shape
    for owner in range(owners):
        for kind in range(2):
            mine = kinds[kind][owner * owned : (owner + 1) * owned, :]
            out_ref[owner, kind] = before_ref[owner, kind] + mine if chained else mine


def add_hist(before, out_shape, bins, labels, elected, parts, shifts, n_feat, cores):
    features = bins.shape[0]
    classes, rows = parts[0].shape
    length = rows // 2
    count = len(parts)
    blocks = 2 * count
    group = min(features, 16)
    chained = before is not None
    vmem = pl.BlockSpec(memory_space=pltpu.VMEM)
    far = pl.BlockSpec(memory_space=pltpu.HBM)
    near = pl.BlockSpec(memory_space=pl.ANY)
    return pl.pallas_call(
        lambda *refs: hist_kernel(group, length, shifts, n_feat, cores, chained, *refs),
        in_specs=[far, far, far] + [near] * count + [vmem] * chained,
        out_specs=vmem,
        scratch_shapes=[
            pltpu.VMEM((features * BINS, 4 * classes), jnp.float32),
            pltpu.VMEM((2, features, length), jnp.int32),
            pltpu.VMEM((blocks, 1, length), jnp.int32),
            pltpu.VMEM((blocks, classes, length), jnp.bfloat16),
            pltpu.VMEM((4 * classes, length), F8),
            pltpu.VMEM((4 * classes, length), F8),
            pltpu.VMEM((4 * classes, 2 * classes), jnp.float32),
            pltpu.VMEM((4 * classes, 2 * classes), jnp.float32),
            pltpu.SemaphoreType.DMA((blocks,)),
            pltpu.SemaphoreType.DMA((blocks,)),
            pltpu.SemaphoreType.DMA((blocks,)),
            pltpu.VMEM(elected.shape, jnp.int32),
            pltpu.SemaphoreType.DMA,
        ],
        out_shape=jax.ShapeDtypeStruct(out_shape, jnp.float32),
        compiler_params=pltpu.CompilerParams(vmem_limit_bytes=48 << 20),
        cost_estimate=pl.CostEstimate(
            flops=2 * count * rows * features * BINS * 4 * classes,
            bytes_accessed=4 * count * rows * features,
            transcendentals=0,
        ),
    )(in_hbm(elected), in_hbm(bins), in_hbm(labels), *parts, *([before] if chained else []))


def gains_kernel(parts_ref, out_ref):
    hist = parts_ref[0]
    for part in range(1, parts_ref.shape[0]):
        hist = hist + parts_ref[part]
    _, owned, width = hist.shape
    hist = hist.reshape(2 * owned, width)
    lane = lax.broadcasted_iota(jnp.int32, hist.shape, 1) % BINS
    shift = 1
    while shift < BINS:
        hist = hist + jnp.where(lane >= shift, pltpu.roll(hist, shift, 1), 0.0)
        shift *= 2
    for e in range(width // BINS):
        left_g = hist[:owned, e * BINS : (e + 1) * BINS]
        left_h = hist[owned:, e * BINS : (e + 1) * BINS]
        tot_g = left_g[:, BINS - 1 :]
        tot_h = left_h[:, BINS - 1 :]
        right_g = tot_g - left_g
        right_h = tot_h - left_h
        gain = 0.5 * (
            left_g * left_g / (left_h + l2_penalty)
            + right_g * right_g / (right_h + l2_penalty)
            - tot_g * tot_g / (tot_h + l2_penalty)
        )
        out_ref[:, e, :] = gain[:, : BINS - 1]


def shards(axis_sizes, scores, labels, bins, elected):
    n_rows, n_feat = axis_sizes
    own_rows, classes = scores.shape
    features = bins.shape[0]
    elect = elected.shape[1]
    owned = classes // n_rows
    labels = labels[None, :]
    cores = 2 if n_feat % 2 == 0 else 1
    chips = n_feat // cores
    swap = [(i, i ^ 1) for i in range(n_feat)]
    coded = score(scores.T, labels)

    def add(hist, parts, shifts):
        shape = (n_rows, 2, owned, elect * BINS)
        return add_hist(hist, shape, bins, labels, elected.T, parts, shifts, n_feat, cores)

    arrived = []
    for turn in range(1, chips):
        around = [(i, (i + turn * cores) % n_feat) for i in range(n_feat)]
        arrived.append(lax.ppermute(coded, "feat", around))
    if cores == 2:
        hist = add(None, [coded, lax.ppermute(coded, "feat", swap)], [(0, 0), (0, 1)])
    else:
        hist = add(None, [coded], [(0, 0)])
    for turn, part in enumerate(arrived, 1):
        part, hist = lax.optimization_barrier((part, hist))
        mate = lax.ppermute(part, "feat", swap) if cores == 2 else None
        hist = add(hist, [part], [(turn, 0)])
        if cores == 2:
            hist = add(hist, [mate], [(turn, 1)])

    if n_rows > 1:
        hist = lax.all_to_all(hist, "rows", 0, 0, tiled=True)
    return pl.pallas_call(
        gains_kernel,
        out_shape=jax.ShapeDtypeStruct((owned, elect, BINS - 1), jnp.float32),
    )(hist)


def solution(mesh):
    sizes = (mesh.shape["rows"], mesh.shape["feat"])
    return jax.shard_map(
        lambda *arrays: shards(sizes, *arrays),
        mesh=mesh,
        in_specs=(P(("rows", "feat"), None), P("rows"), P("feat", "rows"), P(None, "feat")),
        out_specs=P("rows", "feat", None),
        check_vma=False,
    )
```

```python
import jax
import jax.numpy as jnp
from jax import lax
from jax.experimental import pallas as pl
from jax.experimental.pallas import tpu as pltpu
from jax.sharding import PartitionSpec as P

BINS = 64
LANES = 128
l2_penalty = 1.0

SURE = -1e-30

F8 = jnp.float8_e4m3fn
FULL = 256.0
LOW = 16.0


def rounded(x):
    far = x * 65537.0
    return far - (far - x)


def nudged(code, side, wanted):
    code = rounded(code)
    found = rounded(code + side)
    unit = jnp.abs(code) * (1.25 / 256.0)
    return jnp.where(wanted > found, code + unit, jnp.where(wanted < found, code - unit, code))


def score_kernel(n_blocks, scores_ref, labels_ref, coded_ref, score_slots, label_slot, sems):
    rows = scores_ref.shape[1]
    block = rows // n_blocks
    begin = pl.multiple_of(lax.axis_index("feat") * rows, rows)
    label_copy = pltpu.make_async_copy(labels_ref.at[:, pl.ds(begin, rows)], label_slot, sems.at[n_blocks])
    label_copy.start()
    copies = [
        pltpu.make_async_copy(
            scores_ref.at[:, pl.ds(i * block, block)], score_slots.at[:, pl.ds(i * block, block)], sems.at[i]
        )
        for i in range(n_blocks)
    ]
    for copy in copies:
        copy.start()
    label_copy.wait()
    for i in range(n_blocks):
        copies[i].wait()
        where = pl.ds(i * block, block)
        coded_ref[:, where] = encode(score_slots[:, where], label_slot[:, where]).astype(coded_ref.dtype)


def encode(scores, labels):
    is_label = lax.broadcasted_iota(jnp.int32, scores.shape, 0) == labels
    row_max = jnp.max(scores, axis=0, keepdims=True)
    expon = jnp.exp(scores - row_max)
    probs = expon / jnp.sum(expon, axis=0, keepdims=True)
    top = jnp.max(probs, axis=0, keepdims=True)
    labelled = jnp.sum(jnp.where(is_label, probs, 0.0), axis=0, keepdims=True)
    top_code = nudged(jnp.minimum(top - 1.0, SURE), 1.0, rounded(top))
    label_code = jnp.where(
        labelled > 0.5,
        jnp.minimum(labelled - 1.0, SURE),
        nudged(labelled, -1.0, rounded(labelled - 1.0)),
    )
    return jnp.where(is_label, label_code, jnp.where(probs > 0.5, top_code, probs))


def in_hbm(array):
    return pltpu.with_memory_space_constraint(array, pltpu.HBM)


def score(scores, labels):
    classes, rows = scores.shape
    n_blocks = 4
    far = pl.BlockSpec(memory_space=pltpu.HBM)
    return pl.pallas_call(
        lambda *refs: score_kernel(n_blocks, *refs),
        in_specs=[far, far],
        out_specs=pl.BlockSpec(memory_space=pltpu.VMEM),
        scratch_shapes=[
            pltpu.VMEM((classes, rows), jnp.float32),
            pltpu.VMEM((1, rows), jnp.int32),
            pltpu.SemaphoreType.DMA((n_blocks + 1,)),
        ],
        out_shape=jax.ShapeDtypeStruct((classes, rows), jnp.bfloat16),
        compiler_params=pltpu.CompilerParams(vmem_limit_bytes=36 << 20),
        cost_estimate=pl.CostEstimate(
            flops=10 * rows * classes, bytes_accessed=6 * rows * classes, transcendentals=rows * classes
        ),
    )(in_hbm(scores), in_hbm(labels))


def decode(coded, labels, first_class):
    classes, length = coded.shape
    kind = coded.dtype
    class_ids = (lax.broadcasted_iota(jnp.int32, (classes, length), 0) + first_class).astype(kind)
    is_label = class_ids == labels.astype(kind)
    zero, one = jnp.zeros_like(coded), jnp.ones_like(coded)
    above = coded < zero
    side = jnp.where(above, one, -one)
    crossed = is_label != above
    near = jnp.where(crossed, (coded + side) - side, coded)
    whole = jnp.where(crossed, side, zero)
    return near, whole, (near - jnp.abs(coded)) + coded * coded


def power_of_two(values):
    largest = jnp.max(jnp.abs(values), axis=1, keepdims=True).astype(jnp.float32)
    scale = jnp.ones_like(largest)
    back = jnp.ones_like(largest)
    for power in (16, 8, 4, 2, 1):
        small = largest * scale <= 0.5**power
        scale = jnp.where(small, scale * 2.0**power, scale)
        back = jnp.where(small, back * 0.5**power, back)
    return (scale * FULL).astype(values.dtype), back * (1.0 / FULL)


def put_columns(coded_ref, labels, first_class, count, columns_ref, backs_ref):
    classes = coded_ref.shape[0]
    near, whole, square = decode(coded_ref[pl.ds(first_class, count), :], labels, first_class)

    def put(kind, columns, back):
        where = pl.ds(kind * classes + first_class, count)
        columns_ref[where, :] = columns
        backs_ref[where, :] = jnp.broadcast_to(back, (count, backs_ref.shape[1]))

    scale, back = power_of_two(near)
    scaled = near * scale
    high = scaled.astype(F8)
    put(0, high, back)
    put(1, ((scaled - high.astype(scaled.dtype)) * LOW).astype(F8), back * (1.0 / LOW))
    scale, back = power_of_two(square)
    put(2, (square * scale).astype(F8), back)
    put(3, whole.astype(F8), jnp.ones_like(back))


def back_row(backs_ref):
    rows, lanes = backs_ref.shape
    sub = lax.broadcasted_iota(jnp.int32, (lanes, lanes), 0)
    diagonal = sub == lax.broadcasted_iota(jnp.int32, (lanes, lanes), 1)
    parts = [
        jnp.sum(jnp.where(diagonal, backs_ref[start : start + lanes, :], 0.0), axis=0, keepdims=True)
        for start in range(0, rows, lanes)
    ]
    return jnp.concatenate(parts, axis=1)


def add_tile(bins_ref, columns_ref, back, sums_ref, first_feature, count, fresh):
    length = bins_ref.shape[1]
    rows = BINS // 2
    bin_ids = lax.broadcasted_iota(jnp.int32, (rows, length), 0)
    low_ids, high_ids = bin_ids.astype(jnp.int8), (bin_ids + rows).astype(jnp.int8)
    one = jnp.ones((rows, length), F8)
    zero = jnp.zeros((rows, length), F8)
    parts = []
    for offset in range(count):
        codes = jnp.broadcast_to(bins_ref[pl.ds(first_feature + offset, 1), :], (rows, length))
        codes = codes.astype(jnp.int8)
        parts.append(jnp.where(codes == low_ids, one, zero))
        parts.append(jnp.where(codes == high_ids, one, zero))
    added = lax.dot_general(
        jnp.concatenate(parts, axis=0),
        columns_ref[...],
        (((1,), (1,)), ((), ())),
        preferred_element_type=jnp.float32,
    )
    added = added * back
    where = pl.ds(pl.multiple_of(first_feature * BINS, count * BINS), count * BINS)
    if fresh:
        sums_ref[where, :] = added
    else:
        sums_ref[where, :] += added


def hist_kernel(group, length, shifts, n_feat, cores, chained, final, *refs):
    count = len(shifts)
    elect_ref, bins_ref, labels_ref = refs[:3]
    coded_refs = refs[3 : 3 + count]
    refs = refs[3 + count :]
    refs = refs[1:] if chained else refs
    sums_ref, refs = refs[0], refs[1:]
    if final:
        out_ref, refs = refs[0], refs[1:]
    bin_slots, label_slots, coded_slots = refs[:3]
    columns = refs[3:5]
    backs = refs[5:7]
    bin_sems, label_sems, coded_sems, elect_slot, elect_sem = refs[7:]
    classes, rows = coded_refs[0].shape
    features = bins_ref.shape[0]
    place = lax.axis_index("feat")
    halves = rows // length
    blocks = [(part, half) for part in range(count) for half in range(halves)]

    bin_copies, code_copies = [], []
    for index, (part, half) in enumerate(blocks):
        turn, swapped = shifts[part]
        source = (place - turn * cores + n_feat) % n_feat
        if swapped:
            source = source + 1 - 2 * (source % 2)
        begin = pl.multiple_of(source * rows + half * length, length)
        bin_copies.append(
            pltpu.make_async_copy(
                bins_ref.at[:, pl.ds(begin, length)], bin_slots.at[index % 2], bin_sems.at[index]
            )
        )
        code_copies.append(
            (
                pltpu.make_async_copy(
                    coded_refs[part].at[:, pl.ds(half * length, length)],
                    coded_slots.at[index],
                    coded_sems.at[index],
                ),
                pltpu.make_async_copy(
                    labels_ref.at[:, pl.ds(begin, length)], label_slots.at[index], label_sems.at[index]
                ),
            )
        )
    if final:
        elect_copy = pltpu.make_async_copy(elect_ref, elect_slot, elect_sem)
        elect_copy.start()
    for copy in code_copies[0]:
        copy.start()
    bin_copies[0].start()
    bin_copies[1].start()
    for pair in code_copies[1:]:
        for copy in pair:
            copy.start()

    tiles = features // group
    turns = 2 if tiles % 2 == 0 and classes % 64 == 0 else 1
    each = classes // turns
    for copy in code_copies[0]:
        copy.wait()
    put_columns(coded_slots.at[0], label_slots[0], 0, classes, columns[0], backs[0])

    for index in range(len(blocks)):
        now, later = index % 2, (index + 1) % 2
        back = back_row(backs[now])
        bin_copies[index].wait()
        more = index + 1 < len(blocks)
        fresh = index == 0 and not chained
        if more:
            for copy in code_copies[index + 1]:
                copy.wait()

        def one_turn(turn, carry):
            for tile in range(tiles // turns):
                feature = (turn * (tiles // turns) + tile) * group
                add_tile(bin_slots.at[now], columns[now], back, sums_ref, feature, group, fresh)
            if more:
                first = pl.multiple_of(turn * each, each)
                put_columns(
                    coded_slots.at[index + 1], label_slots[index + 1], first, each, columns[later], backs[later]
                )
            return carry

        lax.fori_loop(0, turns, one_turn, 0)
        if index + 2 < len(blocks):
            bin_copies[index + 2].start()

    if not final:
        return
    elect_copy.wait()
    elected = jnp.concatenate([elect_slot[...]] * 4, axis=1) - place * features
    elect = elected.shape[0]

    def pick(feature, picked):
        rows = sums_ref[pl.ds(pl.multiple_of(feature * BINS, BINS), BINS), :]
        return tuple(jnp.where(elected[e : e + 1, :] == feature, rows, picked[e]) for e in range(elect))

    nothing = tuple(jnp.zeros((BINS, 4 * classes), jnp.float32) for _ in range(elect))
    picked = lax.fori_loop(0, features, pick, nothing, unroll=2)
    by_class = jnp.concatenate([part.T for part in picked], axis=1)
    near = by_class[:classes] + by_class[classes : 2 * classes]
    square = by_class[2 * classes : 3 * classes]
    whole = by_class[3 * classes :]
    kinds = (near + whole, near - square)
    owners, _, owned, _ = out_ref.shape
    for owner in range(owners):
        for kind in range(2):
            mine = kinds[kind][owner * owned : (owner + 1) * owned, :]
            out_ref[owner, kind] = mine


def add_hist(before, out_shape, bins, labels, elected, parts, shifts, n_feat, cores):
    features = bins.shape[0]
    classes, rows = parts[0].shape
    length = rows // 2
    count = len(parts)
    blocks = 2 * count
    group = min(features, 16)
    chained = before is not None
    final = out_shape is not None
    vmem = pl.BlockSpec(memory_space=pltpu.VMEM)
    far = pl.BlockSpec(memory_space=pltpu.HBM)
    near = pl.BlockSpec(memory_space=pl.ANY)
    sums = jax.ShapeDtypeStruct((features * BINS, 4 * classes), jnp.float32)
    out = jax.ShapeDtypeStruct(out_shape, jnp.float32) if final else None
    result = pl.pallas_call(
        lambda *refs: hist_kernel(group, length, shifts, n_feat, cores, chained, final, *refs),
        in_specs=[far, far, far] + [near] * count + [vmem] * chained,
        out_specs=[vmem, vmem] if final else [vmem],
        scratch_shapes=[
            pltpu.VMEM((2, features, length), jnp.int32),
            pltpu.VMEM((blocks, 1, length), jnp.int32),
            pltpu.VMEM((blocks, classes, length), jnp.bfloat16),
            pltpu.VMEM((4 * classes, length), F8),
            pltpu.VMEM((4 * classes, length), F8),
            pltpu.VMEM((4 * classes, 2 * classes), jnp.float32),
            pltpu.VMEM((4 * classes, 2 * classes), jnp.float32),
            pltpu.SemaphoreType.DMA((blocks,)),
            pltpu.SemaphoreType.DMA((blocks,)),
            pltpu.SemaphoreType.DMA((blocks,)),
            pltpu.VMEM(elected.shape, jnp.int32),
            pltpu.SemaphoreType.DMA,
        ],
        out_shape=[sums, out] if final else [sums],
        input_output_aliases={3 + count: 0} if chained else {},
        compiler_params=pltpu.CompilerParams(vmem_limit_bytes=36 << 20),
        cost_estimate=pl.CostEstimate(
            flops=2 * count * rows * features * BINS * 4 * classes,
            bytes_accessed=4 * count * rows * features,
            transcendentals=0,
        ),
    )(in_hbm(elected), in_hbm(bins), in_hbm(labels), *parts, *([before] if chained else []))
    return result[-1]


def gains_kernel(parts_ref, out_ref):
    hist = parts_ref[0]
    for part in range(1, parts_ref.shape[0]):
        hist = hist + parts_ref[part]
    _, owned, width = hist.shape
    hist = hist.reshape(2 * owned, width)
    lane = lax.broadcasted_iota(jnp.int32, hist.shape, 1) % BINS
    shift = 1
    while shift < BINS:
        hist = hist + jnp.where(lane >= shift, pltpu.roll(hist, shift, 1), 0.0)
        shift *= 2
    for e in range(width // BINS):
        left_g = hist[:owned, e * BINS : (e + 1) * BINS]
        left_h = hist[owned:, e * BINS : (e + 1) * BINS]
        tot_g = left_g[:, BINS - 1 :]
        tot_h = left_h[:, BINS - 1 :]
        right_g = tot_g - left_g
        right_h = tot_h - left_h
        gain = 0.5 * (
            left_g * left_g / (left_h + l2_penalty)
            + right_g * right_g / (right_h + l2_penalty)
            - tot_g * tot_g / (tot_h + l2_penalty)
        )
        out_ref[:, e, :] = gain[:, : BINS - 1]


def shards(axis_sizes, scores, labels, bins, elected):
    n_rows, n_feat = axis_sizes
    own_rows, classes = scores.shape
    features = bins.shape[0]
    elect = elected.shape[1]
    owned = classes // n_rows
    labels = labels[None, :]
    cores = 2 if n_feat % 2 == 0 else 1
    chips = n_feat // cores
    swap = [(i, i ^ 1) for i in range(n_feat)]
    coded = score(scores.T, labels)

    def add(hist, parts, shifts, last):
        shape = (n_rows, 2, owned, elect * BINS) if last else None
        return add_hist(hist, shape, bins, labels, elected.T, parts, shifts, n_feat, cores)

    arrived = []
    for turn in range(1, chips):
        around = [(i, (i + turn * cores) % n_feat) for i in range(n_feat)]
        arrived.append(lax.ppermute(coded, "feat", around))
    if cores == 2:
        mate = lax.ppermute(coded, "feat", swap)
        hist = add(None, [coded, mate], [(0, 0), (0, 1)], chips == 1)
    else:
        hist = add(None, [coded], [(0, 0)], chips == 1)
    for turn, part in enumerate(arrived, 1):
        last = turn == chips - 1
        part, hist = lax.optimization_barrier((part, hist))
        mate = lax.ppermute(part, "feat", swap) if cores == 2 else None
        hist = add(hist, [part], [(turn, 0)], last and cores == 1)
        if cores == 2:
            hist = add(hist, [mate], [(turn, 1)], last)

    if n_rows > 1:
        hist = lax.all_to_all(hist, "rows", 0, 0, tiled=True)
    return pl.pallas_call(
        gains_kernel,
        out_shape=jax.ShapeDtypeStruct((owned, elect, BINS - 1), jnp.float32),
    )(hist)


def solution(mesh):
    sizes = (mesh.shape["rows"], mesh.shape["feat"])
    return jax.shard_map(
        lambda *arrays: shards(sizes, *arrays),
        mesh=mesh,
        in_specs=(P(("rows", "feat"), None), P("rows"), P("feat", "rows"), P(None, "feat")),
        out_specs=P("rows", "feat", None),
        check_vma=False,
    )
```

```python
import jax
import jax.numpy as jnp
from jax import lax
from jax.experimental import pallas as pl
from jax.experimental.pallas import tpu as pltpu
from jax.sharding import PartitionSpec as P

BINS = 64
LANES = 128
l2_penalty = 1.0

SURE = -1e-30

F8 = jnp.float8_e4m3fn
FULL = 256.0
LOW = 16.0


def rounded(x):
    far = x * 65537.0
    return far - (far - x)


def nudged(code, side, wanted):
    code = rounded(code)
    found = rounded(code + side)
    unit = jnp.abs(code) * (1.25 / 256.0)
    return jnp.where(wanted > found, code + unit, jnp.where(wanted < found, code - unit, code))


def score_kernel(n_blocks, scores_ref, labels_ref, coded_ref, score_slots, label_slot, sems):
    rows = scores_ref.shape[1]
    block = rows // n_blocks
    begin = pl.multiple_of(lax.axis_index("feat") * rows, rows)
    label_copy = pltpu.make_async_copy(labels_ref.at[:, pl.ds(begin, rows)], label_slot, sems.at[n_blocks])
    label_copy.start()
    copies = [
        pltpu.make_async_copy(
            scores_ref.at[:, pl.ds(i * block, block)], score_slots.at[:, pl.ds(i * block, block)], sems.at[i]
        )
        for i in range(n_blocks)
    ]
    for copy in copies:
        copy.start()
    label_copy.wait()
    for i in range(n_blocks):
        copies[i].wait()
        where = pl.ds(i * block, block)
        coded_ref[:, where] = encode(score_slots[:, where], label_slot[:, where]).astype(coded_ref.dtype)


def encode(scores, labels):
    is_label = lax.broadcasted_iota(jnp.int32, scores.shape, 0) == labels
    row_max = jnp.max(scores, axis=0, keepdims=True)
    expon = jnp.exp(scores - row_max)
    top = 1.0 / jnp.sum(expon, axis=0, keepdims=True)
    probs = expon * top
    labelled = jnp.sum(jnp.where(is_label, probs, 0.0), axis=0, keepdims=True)
    top_code = nudged(jnp.minimum(top - 1.0, SURE), 1.0, rounded(top))
    label_code = jnp.where(
        labelled > 0.5,
        jnp.minimum(labelled - 1.0, SURE),
        nudged(labelled, -1.0, rounded(labelled - 1.0)),
    )
    return jnp.where(is_label, label_code, jnp.where(probs > 0.5, top_code, probs))


def in_hbm(array):
    return pltpu.with_memory_space_constraint(array, pltpu.HBM)


def score(scores, labels):
    classes, rows = scores.shape
    n_blocks = 4
    far = pl.BlockSpec(memory_space=pltpu.HBM)
    return pl.pallas_call(
        lambda *refs: score_kernel(n_blocks, *refs),
        in_specs=[far, far],
        out_specs=pl.BlockSpec(memory_space=pltpu.VMEM),
        scratch_shapes=[
            pltpu.VMEM((classes, rows), jnp.float32),
            pltpu.VMEM((1, rows), jnp.int32),
            pltpu.SemaphoreType.DMA((n_blocks + 1,)),
        ],
        out_shape=jax.ShapeDtypeStruct((classes, rows), jnp.bfloat16),
        compiler_params=pltpu.CompilerParams(vmem_limit_bytes=36 << 20),
        cost_estimate=pl.CostEstimate(
            flops=10 * rows * classes, bytes_accessed=6 * rows * classes, transcendentals=rows * classes
        ),
    )(in_hbm(scores), in_hbm(labels))


def decode(coded, labels):
    classes, length = coded.shape
    kind = coded.dtype
    class_ids = lax.broadcasted_iota(jnp.int32, (classes, length), 0).astype(kind)
    is_label = class_ids == labels.astype(kind)
    zero, one = jnp.zeros_like(coded), jnp.ones_like(coded)
    above = coded < zero
    side = jnp.where(above, one, -one)
    crossed = is_label != above
    near = jnp.where(crossed, (coded + side) - side, coded)
    whole = jnp.where(crossed, side, zero)
    return near, whole, (near - jnp.abs(coded)) + coded * coded


def scales(coded):
    largest = jnp.max(jnp.abs(coded), axis=1, keepdims=True).astype(jnp.float32)
    scale = jnp.ones_like(largest)
    back = jnp.ones_like(largest)
    for power in (16, 8, 4, 2, 1):
        small = largest * scale <= 0.5**power
        scale = jnp.where(small, scale * 2.0**power, scale)
        back = jnp.where(small, back * 0.5**power, back)
    return (scale * (FULL / 2)).astype(coded.dtype), back * (2 / FULL)


def put_backs(coded_ref, backs_ref, scales_ref):
    classes = coded_ref.shape[0]
    scale, back = scales(coded_ref[...])
    scales_ref[...] = jnp.broadcast_to(scale, scales_ref.shape)
    for kind, factor in enumerate((back, back * (1.0 / LOW), back, jnp.ones_like(back))):
        backs_ref[kind * classes : (kind + 1) * classes, :] = jnp.broadcast_to(
            factor, (classes, backs_ref.shape[1])
        )


def put_columns(coded_ref, labels_ref, begin, length, columns_ref, scales_ref):
    classes = coded_ref.shape[0]
    rows = pl.ds(begin, length)
    scale = scales_ref[:, :1]
    near, whole, square = decode(coded_ref[:, rows], labels_ref[:, rows])
    scaled = near * scale
    high = scaled.astype(F8)
    low = ((scaled - high.astype(scaled.dtype)) * LOW).astype(F8)
    for kind, part in enumerate((high, low, (square * scale).astype(F8), whole.astype(F8))):
        columns_ref[kind * classes : (kind + 1) * classes, rows] = part


def back_row(backs_ref):
    rows, lanes = backs_ref.shape
    sub = lax.broadcasted_iota(jnp.int32, (lanes, lanes), 0)
    diagonal = sub == lax.broadcasted_iota(jnp.int32, (lanes, lanes), 1)
    parts = [
        jnp.sum(jnp.where(diagonal, backs_ref[start : start + lanes, :], 0.0), axis=0, keepdims=True)
        for start in range(0, rows, lanes)
    ]
    return jnp.concatenate(parts, axis=1)


def add_tile(bins_ref, columns_ref, back, sums_ref, first_feature, count, fresh):
    length = bins_ref.shape[1]
    rows = BINS // 2
    bin_ids = lax.broadcasted_iota(jnp.int32, (rows, length), 0)
    low_ids, high_ids = bin_ids.astype(jnp.int8), (bin_ids + rows).astype(jnp.int8)
    one = jnp.ones((rows, length), F8)
    zero = jnp.zeros((rows, length), F8)
    parts = []
    for offset in range(count):
        codes = jnp.broadcast_to(bins_ref[pl.ds(first_feature + offset, 1), :], (rows, length))
        codes = codes.astype(jnp.int8)
        parts.append(jnp.where(codes == low_ids, one, zero))
        parts.append(jnp.where(codes == high_ids, one, zero))
    added = lax.dot_general(
        jnp.concatenate(parts, axis=0),
        columns_ref[...],
        (((1,), (1,)), ((), ())),
        preferred_element_type=jnp.float32,
    )
    added = added * back
    where = pl.ds(pl.multiple_of(first_feature * BINS, count * BINS), count * BINS)
    if fresh:
        sums_ref[where, :] = added
    else:
        sums_ref[where, :] += added


def hist_kernel(group, length, shifts, n_feat, cores, chained, final, *refs):
    count = len(shifts)
    elect_ref, bins_ref, labels_ref = refs[:3]
    coded_refs = refs[3 : 3 + count]
    refs = refs[3 + count :]
    refs = refs[1:] if chained else refs
    sums_ref, refs = refs[0], refs[1:]
    if final:
        out_ref, refs = refs[0], refs[1:]
    bin_slots, label_slots, coded_slots = refs[:3]
    columns = refs[3:5]
    backs = refs[5:7]
    bin_sems, label_sems, coded_sems, elect_slot, elect_sem, scales_ref = refs[7:]
    classes, rows = coded_refs[0].shape
    features = bins_ref.shape[0]
    place = lax.axis_index("feat")
    halves = rows // length
    blocks = [(part, half) for part in range(count) for half in range(halves)]

    bin_copies, code_copies = [], []
    for index, (part, half) in enumerate(blocks):
        turn, swapped = shifts[part]
        source = (place - turn * cores + n_feat) % n_feat
        if swapped:
            source = source + 1 - 2 * (source % 2)
        begin = pl.multiple_of(source * rows + half * length, length)
        bin_copies.append(
            pltpu.make_async_copy(
                bins_ref.at[:, pl.ds(begin, length)], bin_slots.at[index % 2], bin_sems.at[index]
            )
        )
        code_copies.append(
            (
                pltpu.make_async_copy(
                    coded_refs[part].at[:, pl.ds(half * length, length)],
                    coded_slots.at[index],
                    coded_sems.at[index],
                ),
                pltpu.make_async_copy(
                    labels_ref.at[:, pl.ds(begin, length)], label_slots.at[index], label_sems.at[index]
                ),
            )
        )
    if final:
        elect_copy = pltpu.make_async_copy(elect_ref, elect_slot, elect_sem)
        elect_copy.start()
    for copy in code_copies[0]:
        copy.start()
    bin_copies[0].start()
    bin_copies[1].start()
    for pair in code_copies[1:]:
        for copy in pair:
            copy.start()

    tiles = features // group
    chunk = length // tiles
    for copy in code_copies[0]:
        copy.wait()
    put_backs(coded_slots.at[0], backs[0], scales_ref)
    put_columns(coded_slots.at[0], label_slots.at[0], 0, length, columns[0], scales_ref)

    for index in range(len(blocks)):
        now, later = index % 2, (index + 1) % 2
        back = back_row(backs[now])
        bin_copies[index].wait()
        more = index + 1 < len(blocks)
        fresh = index == 0 and not chained
        if more:
            for copy in code_copies[index + 1]:
                copy.wait()

        if more:
            put_backs(coded_slots.at[index + 1], backs[later], scales_ref)
        for tile in range(tiles):
            add_tile(bin_slots.at[now], columns[now], back, sums_ref, tile * group, group, fresh)
            if more:
                put_columns(
                    coded_slots.at[index + 1],
                    label_slots.at[index + 1],
                    tile * chunk,
                    chunk,
                    columns[later],
                    scales_ref,
                )
        if index + 2 < len(blocks):
            bin_copies[index + 2].start()

    if not final:
        return
    elect_copy.wait()
    width = 2 * classes
    elected = jnp.concatenate([elect_slot[...]] * 2, axis=1) - place * features
    elect = elected.shape[0]
    by_class = []
    for half in range(2):

        def pick(feature, picked):
            rows = sums_ref[
                pl.ds(pl.multiple_of(feature * BINS, BINS), BINS), half * width : (half + 1) * width
            ]
            return tuple(jnp.where(elected[e : e + 1, :] == feature, rows, picked[e]) for e in range(elect))

        nothing = tuple(jnp.zeros((BINS, width), jnp.float32) for _ in range(elect))
        picked = lax.fori_loop(0, features, pick, nothing, unroll=2)
        by_class.append(jnp.concatenate([part.T for part in picked], axis=1))
    near = by_class[0][:classes] + by_class[0][classes:]
    square, whole = by_class[1][:classes], by_class[1][classes:]
    kinds = (near + whole, near - square)
    owners, _, owned, _ = out_ref.shape
    for owner in range(owners):
        for kind in range(2):
            mine = kinds[kind][owner * owned : (owner + 1) * owned, :]
            out_ref[owner, kind] = mine


def add_hist(before, out_shape, bins, labels, elected, parts, shifts, n_feat, cores):
    features = bins.shape[0]
    classes, rows = parts[0].shape
    length = rows // 2
    count = len(parts)
    blocks = 2 * count
    group = min(features, 16)
    chained = before is not None
    final = out_shape is not None
    vmem = pl.BlockSpec(memory_space=pltpu.VMEM)
    far = pl.BlockSpec(memory_space=pltpu.HBM)
    near = pl.BlockSpec(memory_space=pl.ANY)
    sums = jax.ShapeDtypeStruct((features * BINS, 4 * classes), jnp.float32)
    out = jax.ShapeDtypeStruct(out_shape, jnp.float32) if final else None
    result = pl.pallas_call(
        lambda *refs: hist_kernel(group, length, shifts, n_feat, cores, chained, final, *refs),
        in_specs=[far, far, far] + [near] * count + [vmem] * chained,
        out_specs=[vmem, vmem] if final else [vmem],
        scratch_shapes=[
            pltpu.VMEM((2, features, length), jnp.int32),
            pltpu.VMEM((blocks, 1, length), jnp.int32),
            pltpu.VMEM((blocks, classes, length), jnp.bfloat16),
            pltpu.VMEM((4 * classes, length), F8),
            pltpu.VMEM((4 * classes, length), F8),
            pltpu.VMEM((4 * classes, 2 * classes), jnp.float32),
            pltpu.VMEM((4 * classes, 2 * classes), jnp.float32),
            pltpu.SemaphoreType.DMA((blocks,)),
            pltpu.SemaphoreType.DMA((blocks,)),
            pltpu.SemaphoreType.DMA((blocks,)),
            pltpu.VMEM(elected.shape, jnp.int32),
            pltpu.SemaphoreType.DMA,
            pltpu.VMEM((classes, 2 * classes), jnp.bfloat16),
        ],
        out_shape=[sums, out] if final else [sums],
        input_output_aliases={3 + count: 0} if chained else {},
        compiler_params=pltpu.CompilerParams(vmem_limit_bytes=36 << 20),
        cost_estimate=pl.CostEstimate(
            flops=2 * count * rows * features * BINS * 4 * classes,
            bytes_accessed=4 * count * rows * features,
            transcendentals=0,
        ),
    )(in_hbm(elected), in_hbm(bins), in_hbm(labels), *parts, *([before] if chained else []))
    return result[-1]


def gains_kernel(parts_ref, out_ref):
    hist = parts_ref[0]
    for part in range(1, parts_ref.shape[0]):
        hist = hist + parts_ref[part]
    _, owned, width = hist.shape
    hist = hist.reshape(2 * owned, width)
    lane = lax.broadcasted_iota(jnp.int32, hist.shape, 1) % BINS
    left = hist
    after = hist
    shift = 1
    while shift < BINS:
        left = left + jnp.where(lane >= shift, pltpu.roll(left, shift, 1), 0.0)
        after = after + jnp.where(lane < BINS - shift, pltpu.roll(after, width - shift, 1), 0.0)
        shift *= 2
    right = after - hist
    total = left + right
    left_g, left_h = left[:owned], left[owned:]
    right_g, right_h = right[:owned], right[owned:]
    tot_g, tot_h = total[:owned], total[owned:]
    gain = 0.5 * (
        left_g * left_g / (left_h + l2_penalty)
        + right_g * right_g / (right_h + l2_penalty)
        - tot_g * tot_g / (tot_h + l2_penalty)
    )
    for e in range(width // BINS):
        out_ref[:, e, :] = gain[:, e * BINS : (e + 1) * BINS - 1]


def shards(axis_sizes, scores, labels, bins, elected):
    n_rows, n_feat = axis_sizes
    own_rows, classes = scores.shape
    features = bins.shape[0]
    elect = elected.shape[1]
    owned = classes // n_rows
    labels = labels[None, :]
    cores = 2 if n_feat % 2 == 0 else 1
    chips = n_feat // cores
    swap = [(i, i ^ 1) for i in range(n_feat)]
    coded = score(scores.T, labels)

    def add(hist, parts, shifts, last):
        shape = (n_rows, 2, owned, elect * BINS) if last else None
        return add_hist(hist, shape, bins, labels, elected.T, parts, shifts, n_feat, cores)

    arrived = []
    for turn in range(1, chips):
        around = [(i, (i + turn * cores) % n_feat) for i in range(n_feat)]
        arrived.append(lax.ppermute(coded, "feat", around))
    if cores == 2:
        mate = lax.ppermute(coded, "feat", swap)
        hist = add(None, [coded, mate], [(0, 0), (0, 1)], chips == 1)
    else:
        hist = add(None, [coded], [(0, 0)], chips == 1)
    for turn, part in enumerate(arrived, 1):
        last = turn == chips - 1
        part, hist = lax.optimization_barrier((part, hist))
        mate = lax.ppermute(part, "feat", swap) if cores == 2 else None
        hist = add(hist, [part], [(turn, 0)], last and cores == 1)
        if cores == 2:
            hist = add(hist, [mate], [(turn, 1)], last)

    if n_rows > 1:
        hist = lax.all_to_all(hist, "rows", 0, 0, tiled=True)
    return pl.pallas_call(
        gains_kernel,
        out_shape=jax.ShapeDtypeStruct((owned, elect, BINS - 1), jnp.float32),
    )(hist)


def solution(mesh):
    sizes = (mesh.shape["rows"], mesh.shape["feat"])
    return jax.shard_map(
        lambda *arrays: shards(sizes, *arrays),
        mesh=mesh,
        in_specs=(P(("rows", "feat"), None), P("rows"), P("feat", "rows"), P(None, "feat")),
        out_specs=P("rows", "feat", None),
        check_vma=False,
    )
```

```python
import jax
import jax.numpy as jnp
from jax import lax
from jax.experimental import pallas as pl
from jax.experimental.pallas import tpu as pltpu
from jax.sharding import PartitionSpec as P

BINS = 64
l2_penalty = 1.0

SURE = -1e-30

F8 = jnp.float8_e4m3fn
FULL = 256.0
LOW = 16.0


def rounded(x):
    far = x * 65537.0
    return far - (far - x)


def nudged(code, side, wanted):
    code = rounded(code)
    found = rounded(code + side)
    unit = jnp.abs(code) * (1.25 / 256.0)
    return jnp.where(wanted > found, code + unit, jnp.where(wanted < found, code - unit, code))


def score_kernel(n_blocks, scores_ref, labels_ref, coded_ref, score_slots, label_slot, sems):
    rows = scores_ref.shape[1]
    block = rows // n_blocks
    begin = pl.multiple_of(lax.axis_index("feat") * rows, rows)
    label_copy = pltpu.make_async_copy(labels_ref.at[:, pl.ds(begin, rows)], label_slot, sems.at[n_blocks])
    label_copy.start()
    copies = [
        pltpu.make_async_copy(
            scores_ref.at[:, pl.ds(i * block, block)], score_slots.at[:, pl.ds(i * block, block)], sems.at[i]
        )
        for i in range(n_blocks)
    ]
    for copy in copies:
        copy.start()
    label_copy.wait()
    for i in range(n_blocks):
        copies[i].wait()
        where = pl.ds(i * block, block)
        coded_ref[:, where] = encode(score_slots[:, where], label_slot[:, where]).astype(coded_ref.dtype)


def encode(scores, labels):
    is_label = lax.broadcasted_iota(jnp.int32, scores.shape, 0) == labels
    row_max = jnp.max(scores, axis=0, keepdims=True)
    expon = jnp.exp(scores - row_max)
    top = 1.0 / jnp.sum(expon, axis=0, keepdims=True)
    probs = expon * top
    labelled = jnp.sum(jnp.where(is_label, probs, 0.0), axis=0, keepdims=True)
    top_code = nudged(jnp.minimum(top - 1.0, SURE), 1.0, rounded(top))
    label_code = jnp.where(
        labelled > 0.5,
        jnp.minimum(labelled - 1.0, SURE),
        nudged(labelled, -1.0, rounded(labelled - 1.0)),
    )
    return jnp.where(is_label, label_code, jnp.where(probs > 0.5, top_code, probs))


def in_hbm(array):
    return pltpu.with_memory_space_constraint(array, pltpu.HBM)


def score(scores, labels):
    classes, rows = scores.shape
    n_blocks = 4
    far = pl.BlockSpec(memory_space=pltpu.HBM)
    return pl.pallas_call(
        lambda *refs: score_kernel(n_blocks, *refs),
        in_specs=[far, far],
        out_specs=pl.BlockSpec(memory_space=pltpu.VMEM),
        scratch_shapes=[
            pltpu.VMEM((classes, rows), jnp.float32),
            pltpu.VMEM((1, rows), jnp.int32),
            pltpu.SemaphoreType.DMA((n_blocks + 1,)),
        ],
        out_shape=jax.ShapeDtypeStruct((classes, rows), jnp.bfloat16),
        compiler_params=pltpu.CompilerParams(vmem_limit_bytes=36 << 20),
        cost_estimate=pl.CostEstimate(
            flops=10 * rows * classes, bytes_accessed=6 * rows * classes, transcendentals=rows * classes
        ),
    )(in_hbm(scores), in_hbm(labels))


def decode(coded, labels):
    classes, length = coded.shape
    kind = coded.dtype
    class_ids = lax.broadcasted_iota(jnp.int32, (classes, length), 0).astype(kind)
    is_label = class_ids == labels.astype(kind)
    zero, one = jnp.zeros_like(coded), jnp.ones_like(coded)
    above = coded < zero
    side = jnp.where(above, one, -one)
    crossed = is_label != above
    near = jnp.where(crossed, (coded + side) - side, coded)
    whole = jnp.where(crossed, side, zero)
    return near, whole, (near - jnp.abs(coded)) + coded * coded


def scales(coded):
    largest = jnp.max(jnp.abs(coded), axis=1, keepdims=True).astype(jnp.float32)
    scale = jnp.ones_like(largest)
    back = jnp.ones_like(largest)
    for power in (16, 8, 4, 2, 1):
        small = largest * scale <= 0.5**power
        scale = jnp.where(small, scale * 2.0**power, scale)
        back = jnp.where(small, back * 0.5**power, back)
    return (scale * (FULL / 2)).astype(coded.dtype), back * (2 / FULL)


def put_backs(coded_ref, backs_ref, scales_ref):
    classes = coded_ref.shape[0]
    scale, back = scales(coded_ref[...])
    scales_ref[...] = jnp.broadcast_to(scale, scales_ref.shape)
    for kind, factor in enumerate((back, back * (1.0 / LOW), back, jnp.ones_like(back))):
        backs_ref[kind * classes : (kind + 1) * classes, :] = jnp.broadcast_to(
            factor, (classes, backs_ref.shape[1])
        )


def put_columns(coded_ref, labels_ref, begin, length, columns_ref, scales_ref):
    classes = coded_ref.shape[0]
    rows = pl.ds(begin, length)
    scale = scales_ref[:, :1]
    near, whole, square = decode(coded_ref[:, rows], labels_ref[:, rows])
    scaled = near * scale
    high = scaled.astype(F8)
    low = ((scaled - high.astype(scaled.dtype)) * LOW).astype(F8)
    for kind, part in enumerate((high, low, (square * scale).astype(F8), whole.astype(F8))):
        columns_ref[kind * classes : (kind + 1) * classes, rows] = part


def back_row(backs_ref):
    rows, lanes = backs_ref.shape
    sub = lax.broadcasted_iota(jnp.int32, (lanes, lanes), 0)
    diagonal = sub == lax.broadcasted_iota(jnp.int32, (lanes, lanes), 1)
    parts = [
        jnp.sum(jnp.where(diagonal, backs_ref[start : start + lanes, :], 0.0), axis=0, keepdims=True)
        for start in range(0, rows, lanes)
    ]
    return jnp.concatenate(parts, axis=1)


def add_tile(bins_ref, columns_ref, back, sums_ref, first_feature, count, fresh):
    length = bins_ref.shape[1]
    rows = BINS // 2
    bin_ids = lax.broadcasted_iota(jnp.int32, (rows, length), 0)
    low_ids, high_ids = bin_ids.astype(jnp.int8), (bin_ids + rows).astype(jnp.int8)
    one = jnp.ones((rows, length), F8)
    zero = jnp.zeros((rows, length), F8)
    parts = []
    for offset in range(count):
        codes = jnp.broadcast_to(bins_ref[pl.ds(first_feature + offset, 1), :], (rows, length))
        codes = codes.astype(jnp.int8)
        parts.append(jnp.where(codes == low_ids, one, zero))
        parts.append(jnp.where(codes == high_ids, one, zero))
    added = lax.dot_general(
        jnp.concatenate(parts, axis=0),
        columns_ref[...],
        (((1,), (1,)), ((), ())),
        preferred_element_type=jnp.float32,
    )
    added = added * back
    where = pl.ds(pl.multiple_of(first_feature * BINS, count * BINS), count * BINS)
    if fresh:
        sums_ref[where, :] = added
    else:
        sums_ref[where, :] += added


def hist_kernel(group, length, shifts, n_feat, cores, chained, final, *refs):
    count = len(shifts)
    elect_ref, bins_ref, labels_ref = refs[:3]
    coded_refs = refs[3 : 3 + count]
    refs = refs[3 + count :]
    refs = refs[1:] if chained else refs
    sums_ref, refs = refs[0], refs[1:]
    if final:
        out_ref, refs = refs[0], refs[1:]
    bin_slots, label_slots, coded_slots = refs[:3]
    columns = refs[3:5]
    backs = refs[5:7]
    bin_sems, label_sems, coded_sems, elect_slot, elect_sem, scales_ref = refs[7:]
    classes, rows = coded_refs[0].shape
    features = bins_ref.shape[0]
    place = lax.axis_index("feat")
    halves = rows // length
    blocks = [(part, half) for part in range(count) for half in range(halves)]

    bin_copies, code_copies = [], []
    for index, (part, half) in enumerate(blocks):
        turn, swapped = shifts[part]
        source = (place - turn * cores + n_feat) % n_feat
        if swapped:
            source = source + 1 - 2 * (source % 2)
        begin = pl.multiple_of(source * rows + half * length, length)
        bin_copies.append(
            pltpu.make_async_copy(
                bins_ref.at[:, pl.ds(begin, length)], bin_slots.at[index % 2], bin_sems.at[index]
            )
        )
        code_copies.append(
            (
                pltpu.make_async_copy(
                    coded_refs[part].at[:, pl.ds(half * length, length)],
                    coded_slots.at[index],
                    coded_sems.at[index],
                ),
                pltpu.make_async_copy(
                    labels_ref.at[:, pl.ds(begin, length)], label_slots.at[index], label_sems.at[index]
                ),
            )
        )
    if final:
        elect_copy = pltpu.make_async_copy(elect_ref, elect_slot, elect_sem)
        elect_copy.start()
    for copy in code_copies[0]:
        copy.start()
    bin_copies[0].start()
    bin_copies[1].start()
    for pair in code_copies[1:]:
        for copy in pair:
            copy.start()

    tiles = features // group
    turns = 2 if len(blocks) > 2 and tiles % 2 == 0 else 1
    chunk = length // tiles
    for copy in code_copies[0]:
        copy.wait()
    put_backs(coded_slots.at[0], backs[0], scales_ref)
    put_columns(coded_slots.at[0], label_slots.at[0], 0, length, columns[0], scales_ref)

    for index in range(len(blocks)):
        now, later = index % 2, (index + 1) % 2
        back = back_row(backs[now])
        bin_copies[index].wait()
        more = index + 1 < len(blocks)
        fresh = index == 0 and not chained
        if more:
            for copy in code_copies[index + 1]:
                copy.wait()

        if more:
            put_backs(coded_slots.at[index + 1], backs[later], scales_ref)

        def one_turn(turn, carry):
            for offset in range(tiles // turns):
                tile = turn * (tiles // turns) + offset
                add_tile(bin_slots.at[now], columns[now], back, sums_ref, tile * group, group, fresh)
                if more:
                    put_columns(
                        coded_slots.at[index + 1],
                        label_slots.at[index + 1],
                        pl.multiple_of(tile * chunk, chunk),
                        chunk,
                        columns[later],
                        scales_ref,
                    )
            return carry

        if turns == 1:
            one_turn(0, 0)
        else:
            lax.fori_loop(0, turns, one_turn, 0)
        if index + 2 < len(blocks):
            bin_copies[index + 2].start()

    if not final:
        return
    elect_copy.wait()
    width = 2 * classes
    elected = jnp.concatenate([elect_slot[...]] * 2, axis=1) - place * features
    elect = elected.shape[0]
    by_class = []
    for half in range(2):

        def pick(feature, picked):
            rows = sums_ref[
                pl.ds(pl.multiple_of(feature * BINS, BINS), BINS), half * width : (half + 1) * width
            ]
            return tuple(jnp.where(elected[e : e + 1, :] == feature, rows, picked[e]) for e in range(elect))

        nothing = tuple(jnp.zeros((BINS, width), jnp.float32) for _ in range(elect))
        picked = lax.fori_loop(0, features, pick, nothing, unroll=2)
        by_class.append(jnp.concatenate([part.T for part in picked], axis=1))
    near = by_class[0][:classes] + by_class[0][classes:]
    square, whole = by_class[1][:classes], by_class[1][classes:]
    kinds = (near + whole, near - square)
    owners, _, owned, _ = out_ref.shape
    for owner in range(owners):
        for kind in range(2):
            mine = kinds[kind][owner * owned : (owner + 1) * owned, :]
            out_ref[owner, kind] = mine


def add_hist(before, out_shape, bins, labels, elected, parts, shifts, n_feat, cores):
    features = bins.shape[0]
    classes, rows = parts[0].shape
    length = rows // 2
    count = len(parts)
    blocks = 2 * count
    group = min(features, 16)
    chained = before is not None
    final = out_shape is not None
    vmem = pl.BlockSpec(memory_space=pltpu.VMEM)
    far = pl.BlockSpec(memory_space=pltpu.HBM)
    near = pl.BlockSpec(memory_space=pl.ANY)
    sums = jax.ShapeDtypeStruct((features * BINS, 4 * classes), jnp.float32)
    out = jax.ShapeDtypeStruct(out_shape, jnp.float32) if final else None
    result = pl.pallas_call(
        lambda *refs: hist_kernel(group, length, shifts, n_feat, cores, chained, final, *refs),
        in_specs=[far, far, far] + [near] * count + [vmem] * chained,
        out_specs=[vmem, vmem] if final else [vmem],
        scratch_shapes=[
            pltpu.VMEM((2, features, length), jnp.int32),
            pltpu.VMEM((blocks, 1, length), jnp.int32),
            pltpu.VMEM((blocks, classes, length), jnp.bfloat16),
            pltpu.VMEM((4 * classes, length), F8),
            pltpu.VMEM((4 * classes, length), F8),
            pltpu.VMEM((4 * classes, 2 * classes), jnp.float32),
            pltpu.VMEM((4 * classes, 2 * classes), jnp.float32),
            pltpu.SemaphoreType.DMA((blocks,)),
            pltpu.SemaphoreType.DMA((blocks,)),
            pltpu.SemaphoreType.DMA((blocks,)),
            pltpu.VMEM(elected.shape, jnp.int32),
            pltpu.SemaphoreType.DMA,
            pltpu.VMEM((classes, 2 * classes), jnp.bfloat16),
        ],
        out_shape=[sums, out] if final else [sums],
        input_output_aliases={3 + count: 0} if chained else {},
        compiler_params=pltpu.CompilerParams(vmem_limit_bytes=36 << 20),
        cost_estimate=pl.CostEstimate(
            flops=2 * count * rows * features * BINS * 4 * classes,
            bytes_accessed=4 * count * rows * features,
            transcendentals=0,
        ),
    )(in_hbm(elected), in_hbm(bins), in_hbm(labels), *parts, *([before] if chained else []))
    return result[-1]


def gains_kernel(parts_ref, out_ref):
    hist = parts_ref[0]
    for part in range(1, parts_ref.shape[0]):
        hist = hist + parts_ref[part]
    _, owned, width = hist.shape
    hist = hist.reshape(2 * owned, width)
    lane = lax.broadcasted_iota(jnp.int32, hist.shape, 1) % BINS
    left = hist
    after = hist
    shift = 1
    while shift < BINS:
        left = left + jnp.where(lane >= shift, pltpu.roll(left, shift, 1), 0.0)
        after = after + jnp.where(lane < BINS - shift, pltpu.roll(after, width - shift, 1), 0.0)
        shift *= 2
    right = after - hist
    total = left + right
    left_g, left_h = left[:owned], left[owned:]
    right_g, right_h = right[:owned], right[owned:]
    tot_g, tot_h = total[:owned], total[owned:]
    gain = 0.5 * (
        left_g * left_g / (left_h + l2_penalty)
        + right_g * right_g / (right_h + l2_penalty)
        - tot_g * tot_g / (tot_h + l2_penalty)
    )
    for e in range(width // BINS):
        out_ref[:, e, :] = gain[:, e * BINS : (e + 1) * BINS - 1]


def shards(axis_sizes, scores, labels, bins, elected):
    n_rows, n_feat = axis_sizes
    own_rows, classes = scores.shape
    features = bins.shape[0]
    elect = elected.shape[1]
    owned = classes // n_rows
    labels = labels[None, :]
    cores = 2 if n_feat % 2 == 0 else 1
    chips = n_feat // cores
    swap = [(i, i ^ 1) for i in range(n_feat)]
    coded = score(scores.T, labels)

    def add(hist, parts, shifts, last):
        shape = (n_rows, 2, owned, elect * BINS) if last else None
        return add_hist(hist, shape, bins, labels, elected.T, parts, shifts, n_feat, cores)

    arrived = []
    for turn in range(1, chips):
        around = [(i, (i + turn * cores) % n_feat) for i in range(n_feat)]
        arrived.append(lax.ppermute(coded, "feat", around))
    if cores == 2:
        mate = lax.ppermute(coded, "feat", swap)
        hist = add(None, [coded, mate], [(0, 0), (0, 1)], chips == 1)
    else:
        hist = add(None, [coded], [(0, 0)], chips == 1)
    for turn, part in enumerate(arrived, 1):
        last = turn == chips - 1
        part, hist = lax.optimization_barrier((part, hist))
        mate = lax.ppermute(part, "feat", swap) if cores == 2 else None
        hist = add(hist, [part], [(turn, 0)], last and cores == 1)
        if cores == 2:
            hist = add(hist, [mate], [(turn, 1)], last)

    if n_rows > 1:
        hist = lax.all_to_all(hist, "rows", 0, 0, tiled=True)
    return pl.pallas_call(
        gains_kernel,
        out_shape=jax.ShapeDtypeStruct((owned, elect, BINS - 1), jnp.float32),
    )(hist)


def solution(mesh):
    sizes = (mesh.shape["rows"], mesh.shape["feat"])
    return jax.shard_map(
        lambda *arrays: shards(sizes, *arrays),
        mesh=mesh,
        in_specs=(P(("rows", "feat"), None), P("rows"), P("feat", "rows"), P(None, "feat")),
        out_specs=P("rows", "feat", None),
        check_vma=False,
    )
```

```python
import jax
import jax.numpy as jnp
from jax import lax
from jax.experimental import pallas as pl
from jax.experimental.pallas import tpu as pltpu
from jax.sharding import PartitionSpec as P

BINS = 64
l2_penalty = 1.0

SURE = -1e-30

F8 = jnp.float8_e4m3fn
FULL = 256.0
LOW = 16.0


def rounded(x):
    far = x * 65537.0
    return far - (far - x)


def nudged(code, side, wanted):
    code = rounded(code)
    found = rounded(code + side)
    unit = jnp.abs(code) * (1.25 / 256.0)
    return jnp.where(wanted > found, code + unit, jnp.where(wanted < found, code - unit, code))


def score_kernel(n_blocks, scores_ref, labels_ref, coded_ref, score_slots, label_slot, sems):
    rows = scores_ref.shape[1]
    block = rows // n_blocks
    begin = pl.multiple_of(lax.axis_index("feat") * rows, rows)
    label_copy = pltpu.make_async_copy(labels_ref.at[:, pl.ds(begin, rows)], label_slot, sems.at[n_blocks])
    label_copy.start()
    copies = [
        pltpu.make_async_copy(
            scores_ref.at[:, pl.ds(i * block, block)], score_slots.at[:, pl.ds(i * block, block)], sems.at[i]
        )
        for i in range(n_blocks)
    ]
    for copy in copies:
        copy.start()
    label_copy.wait()
    for i in range(n_blocks):
        copies[i].wait()
        where = pl.ds(i * block, block)
        coded_ref[:, where] = encode(score_slots[:, where], label_slot[:, where]).astype(coded_ref.dtype)


def encode(scores, labels):
    is_label = lax.broadcasted_iota(jnp.int32, scores.shape, 0) == labels
    row_max = jnp.max(scores, axis=0, keepdims=True)
    expon = jnp.exp(scores - row_max)
    top = 1.0 / jnp.sum(expon, axis=0, keepdims=True)
    probs = expon * top
    labelled = jnp.sum(jnp.where(is_label, probs, 0.0), axis=0, keepdims=True)
    top_code = nudged(jnp.minimum(top - 1.0, SURE), 1.0, rounded(top))
    label_code = jnp.where(
        labelled > 0.5,
        jnp.minimum(labelled - 1.0, SURE),
        nudged(labelled, -1.0, rounded(labelled - 1.0)),
    )
    return jnp.where(is_label, label_code, jnp.where(probs > 0.5, top_code, probs))


def in_hbm(array):
    return pltpu.with_memory_space_constraint(array, pltpu.HBM)


def score(scores, labels):
    classes, rows = scores.shape
    n_blocks = 8
    far = pl.BlockSpec(memory_space=pltpu.HBM)
    return pl.pallas_call(
        lambda *refs: score_kernel(n_blocks, *refs),
        in_specs=[far, far],
        out_specs=pl.BlockSpec(memory_space=pltpu.VMEM),
        scratch_shapes=[
            pltpu.VMEM((classes, rows), jnp.float32),
            pltpu.VMEM((1, rows), jnp.int32),
            pltpu.SemaphoreType.DMA((n_blocks + 1,)),
        ],
        out_shape=jax.ShapeDtypeStruct((classes, rows), jnp.bfloat16),
        compiler_params=pltpu.CompilerParams(vmem_limit_bytes=36 << 20),
        cost_estimate=pl.CostEstimate(
            flops=10 * rows * classes, bytes_accessed=6 * rows * classes, transcendentals=rows * classes
        ),
    )(in_hbm(scores), in_hbm(labels))


def decode(coded, labels):
    classes, length = coded.shape
    kind = coded.dtype
    class_ids = lax.broadcasted_iota(jnp.int32, (classes, length), 0).astype(kind)
    is_label = class_ids == labels.astype(kind)
    zero, one = jnp.zeros_like(coded), jnp.ones_like(coded)
    above = coded < zero
    side = jnp.where(above, one, -one)
    crossed = is_label != above
    near = jnp.where(crossed, (coded + side) - side, coded)
    whole = jnp.where(crossed, side, zero)
    return near, whole, (near - jnp.abs(coded)) + coded * coded


def scales(coded):
    largest = jnp.max(jnp.abs(coded), axis=1, keepdims=True).astype(jnp.float32)
    scale = jnp.ones_like(largest)
    back = jnp.ones_like(largest)
    for power in (16, 8, 4, 2, 1):
        small = largest * scale <= 0.5**power
        scale = jnp.where(small, scale * 2.0**power, scale)
        back = jnp.where(small, back * 0.5**power, back)
    return (scale * (FULL / 2)).astype(coded.dtype), back * (2 / FULL)


def put_backs(coded_ref, backs_ref, scales_ref):
    classes = coded_ref.shape[0]
    scale, back = scales(coded_ref[...])
    scales_ref[...] = jnp.broadcast_to(scale, scales_ref.shape)
    for kind, factor in enumerate((back, back * (1.0 / LOW), back, jnp.ones_like(back))):
        backs_ref[kind * classes : (kind + 1) * classes, :] = jnp.broadcast_to(
            factor, (classes, backs_ref.shape[1])
        )


def put_columns(coded_ref, labels_ref, begin, length, columns_ref, scales_ref):
    classes = coded_ref.shape[0]
    rows = pl.ds(begin, length)
    scale = scales_ref[:, :1]
    near, whole, square = decode(coded_ref[:, rows], labels_ref[:, rows])
    scaled = near * scale
    high = scaled.astype(F8)
    low = ((scaled - high.astype(scaled.dtype)) * LOW).astype(F8)
    for kind, part in enumerate((high, low, (square * scale).astype(F8), whole.astype(F8))):
        columns_ref[kind * classes : (kind + 1) * classes, rows] = part


def back_row(backs_ref):
    rows, lanes = backs_ref.shape
    sub = lax.broadcasted_iota(jnp.int32, (lanes, lanes), 0)
    diagonal = sub == lax.broadcasted_iota(jnp.int32, (lanes, lanes), 1)
    parts = [
        jnp.sum(jnp.where(diagonal, backs_ref[start : start + lanes, :], 0.0), axis=0, keepdims=True)
        for start in range(0, rows, lanes)
    ]
    return jnp.concatenate(parts, axis=1)


def add_tile(bins_ref, columns_ref, back, sums_ref, first_feature, count, fresh):
    length = bins_ref.shape[1]
    rows = BINS // 2
    bin_ids = lax.broadcasted_iota(jnp.int32, (rows, length), 0)
    low_ids, high_ids = bin_ids.astype(jnp.int8), (bin_ids + rows).astype(jnp.int8)
    one = jnp.ones((rows, length), F8)
    zero = jnp.zeros((rows, length), F8)
    parts = []
    for offset in range(count):
        codes = jnp.broadcast_to(bins_ref[pl.ds(first_feature + offset, 1), :], (rows, length))
        codes = codes.astype(jnp.int8)
        parts.append(jnp.where(codes == low_ids, one, zero))
        parts.append(jnp.where(codes == high_ids, one, zero))
    added = lax.dot_general(
        jnp.concatenate(parts, axis=0),
        columns_ref[...],
        (((1,), (1,)), ((), ())),
        preferred_element_type=jnp.float32,
    )
    added = added * back
    where = pl.ds(pl.multiple_of(first_feature * BINS, count * BINS), count * BINS)
    if fresh:
        sums_ref[where, :] = added
    else:
        sums_ref[where, :] += added


def hist_kernel(group, length, shifts, n_feat, cores, chained, final, *refs):
    count = len(shifts)
    elect_ref, bins_ref, labels_ref = refs[:3]
    coded_refs = refs[3 : 3 + count]
    refs = refs[3 + count :]
    refs = refs[1:] if chained else refs
    sums_ref, refs = refs[0], refs[1:]
    if final:
        out_ref, refs = refs[0], refs[1:]
    bin_slots, label_slots, coded_slots = refs[:3]
    columns = refs[3:5]
    backs = refs[5:7]
    bin_sems, label_sems, coded_sems, elect_slot, elect_sem, scales_ref = refs[7:]
    classes, rows = coded_refs[0].shape
    features = bins_ref.shape[0]
    place = lax.axis_index("feat")
    halves = rows // length
    blocks = [(part, half) for part in range(count) for half in range(halves)]

    bin_copies, code_copies = [], []
    for index, (part, half) in enumerate(blocks):
        turn, swapped = shifts[part]
        source = (place - turn * cores + n_feat) % n_feat
        if swapped:
            source = source + 1 - 2 * (source % 2)
        begin = pl.multiple_of(source * rows + half * length, length)
        bin_copies.append(
            pltpu.make_async_copy(
                bins_ref.at[:, pl.ds(begin, length)], bin_slots.at[index % 2], bin_sems.at[index]
            )
        )
        code_copies.append(
            (
                pltpu.make_async_copy(
                    coded_refs[part].at[:, pl.ds(half * length, length)],
                    coded_slots.at[index],
                    coded_sems.at[index],
                ),
                pltpu.make_async_copy(
                    labels_ref.at[:, pl.ds(begin, length)], label_slots.at[index], label_sems.at[index]
                ),
            )
        )
    if final:
        elect_copy = pltpu.make_async_copy(elect_ref, elect_slot, elect_sem)
        elect_copy.start()
    for copy in code_copies[0]:
        copy.start()
    bin_copies[0].start()
    bin_copies[1].start()
    for pair in code_copies[1:]:
        for copy in pair:
            copy.start()

    tiles = features // group
    turns = 2 if len(blocks) > 2 and tiles % 2 == 0 else 1
    chunk = length // tiles
    for copy in code_copies[0]:
        copy.wait()
    put_backs(coded_slots.at[0], backs[0], scales_ref)
    put_columns(coded_slots.at[0], label_slots.at[0], 0, length, columns[0], scales_ref)

    for index in range(len(blocks)):
        now, later = index % 2, (index + 1) % 2
        back = back_row(backs[now])
        bin_copies[index].wait()
        more = index + 1 < len(blocks)
        fresh = index == 0 and not chained
        if more:
            for copy in code_copies[index + 1]:
                copy.wait()

        if more:
            put_backs(coded_slots.at[index + 1], backs[later], scales_ref)

        def one_turn(turn, carry):
            for offset in range(tiles // turns):
                tile = turn * (tiles // turns) + offset
                add_tile(bin_slots.at[now], columns[now], back, sums_ref, tile * group, group, fresh)
                if more:
                    put_columns(
                        coded_slots.at[index + 1],
                        label_slots.at[index + 1],
                        pl.multiple_of(tile * chunk, chunk),
                        chunk,
                        columns[later],
                        scales_ref,
                    )
            return carry

        if turns == 1:
            one_turn(0, 0)
        else:
            lax.fori_loop(0, turns, one_turn, 0)
        if index + 2 < len(blocks):
            bin_copies[index + 2].start()

    if not final:
        return
    elect_copy.wait()
    width = 2 * classes
    elected = jnp.concatenate([elect_slot[...]] * 2, axis=1) - place * features
    elect = elected.shape[0]
    by_class = []
    for half in range(2):

        def pick(feature, picked):
            rows = sums_ref[
                pl.ds(pl.multiple_of(feature * BINS, BINS), BINS), half * width : (half + 1) * width
            ]
            return tuple(jnp.where(elected[e : e + 1, :] == feature, rows, picked[e]) for e in range(elect))

        nothing = tuple(jnp.zeros((BINS, width), jnp.float32) for _ in range(elect))
        picked = lax.fori_loop(0, features, pick, nothing, unroll=8)
        by_class.append(jnp.concatenate([part.T for part in picked], axis=1))
    near = by_class[0][:classes] + by_class[0][classes:]
    square, whole = by_class[1][:classes], by_class[1][classes:]
    kinds = (near + whole, near - square)
    owners, _, owned, _ = out_ref.shape
    for owner in range(owners):
        for kind in range(2):
            mine = kinds[kind][owner * owned : (owner + 1) * owned, :]
            out_ref[owner, kind] = mine


def add_hist(before, out_shape, bins, labels, elected, parts, shifts, n_feat, cores):
    features = bins.shape[0]
    classes, rows = parts[0].shape
    length = rows // 2
    count = len(parts)
    blocks = 2 * count
    group = min(features, 16)
    chained = before is not None
    final = out_shape is not None
    vmem = pl.BlockSpec(memory_space=pltpu.VMEM)
    far = pl.BlockSpec(memory_space=pltpu.HBM)
    near = pl.BlockSpec(memory_space=pl.ANY)
    sums = jax.ShapeDtypeStruct((features * BINS, 4 * classes), jnp.float32)
    out = jax.ShapeDtypeStruct(out_shape, jnp.float32) if final else None
    result = pl.pallas_call(
        lambda *refs: hist_kernel(group, length, shifts, n_feat, cores, chained, final, *refs),
        in_specs=[far, far, far] + [near] * count + [vmem] * chained,
        out_specs=[vmem, vmem] if final else [vmem],
        scratch_shapes=[
            pltpu.VMEM((2, features, length), jnp.int32),
            pltpu.VMEM((blocks, 1, length), jnp.int32),
            pltpu.VMEM((blocks, classes, length), jnp.bfloat16),
            pltpu.VMEM((4 * classes, length), F8),
            pltpu.VMEM((4 * classes, length), F8),
            pltpu.VMEM((4 * classes, 2 * classes), jnp.float32),
            pltpu.VMEM((4 * classes, 2 * classes), jnp.float32),
            pltpu.SemaphoreType.DMA((blocks,)),
            pltpu.SemaphoreType.DMA((blocks,)),
            pltpu.SemaphoreType.DMA((blocks,)),
            pltpu.VMEM(elected.shape, jnp.int32),
            pltpu.SemaphoreType.DMA,
            pltpu.VMEM((classes, 2 * classes), jnp.bfloat16),
        ],
        out_shape=[sums, out] if final else [sums],
        input_output_aliases={3 + count: 0} if chained else {},
        compiler_params=pltpu.CompilerParams(vmem_limit_bytes=36 << 20),
        cost_estimate=pl.CostEstimate(
            flops=2 * count * rows * features * BINS * 4 * classes,
            bytes_accessed=4 * count * rows * features,
            transcendentals=0,
        ),
    )(in_hbm(elected), in_hbm(bins), in_hbm(labels), *parts, *([before] if chained else []))
    return result[-1]


def gains_kernel(parts_ref, out_ref):
    hist = parts_ref[0]
    for part in range(1, parts_ref.shape[0]):
        hist = hist + parts_ref[part]
    _, owned, width = hist.shape
    hist = hist.reshape(2 * owned, width)
    lane = lax.broadcasted_iota(jnp.int32, hist.shape, 1) % BINS
    left = hist
    after = hist
    shift = 1
    while shift < BINS:
        left = left + jnp.where(lane >= shift, pltpu.roll(left, shift, 1), 0.0)
        after = after + jnp.where(lane < BINS - shift, pltpu.roll(after, width - shift, 1), 0.0)
        shift *= 2
    right = after - hist
    total = left + right
    left_g, left_h = left[:owned], left[owned:]
    right_g, right_h = right[:owned], right[owned:]
    tot_g, tot_h = total[:owned], total[owned:]
    gain = 0.5 * (
        left_g * left_g / (left_h + l2_penalty)
        + right_g * right_g / (right_h + l2_penalty)
        - tot_g * tot_g / (tot_h + l2_penalty)
    )
    for e in range(width // BINS):
        out_ref[:, e, :] = gain[:, e * BINS : (e + 1) * BINS - 1]


def shards(axis_sizes, scores, labels, bins, elected):
    n_rows, n_feat = axis_sizes
    own_rows, classes = scores.shape
    features = bins.shape[0]
    elect = elected.shape[1]
    owned = classes // n_rows
    labels = labels[None, :]
    cores = 2 if n_feat % 2 == 0 else 1
    chips = n_feat // cores
    swap = [(i, i ^ 1) for i in range(n_feat)]
    coded = score(scores.T, labels)

    def add(hist, parts, shifts, last):
        shape = (n_rows, 2, owned, elect * BINS) if last else None
        return add_hist(hist, shape, bins, labels, elected.T, parts, shifts, n_feat, cores)

    arrived = []
    for turn in range(1, chips):
        around = [(i, (i + turn * cores) % n_feat) for i in range(n_feat)]
        arrived.append(lax.ppermute(coded, "feat", around))
    if cores == 2:
        mate = lax.ppermute(coded, "feat", swap)
        hist = add(None, [coded, mate], [(0, 0), (0, 1)], chips == 1)
    else:
        hist = add(None, [coded], [(0, 0)], chips == 1)
    for turn, part in enumerate(arrived, 1):
        last = turn == chips - 1
        part, hist = lax.optimization_barrier((part, hist))
        mate = lax.ppermute(part, "feat", swap) if cores == 2 else None
        hist = add(hist, [part], [(turn, 0)], last and cores == 1)
        if cores == 2:
            hist = add(hist, [mate], [(turn, 1)], last)

    if n_rows > 1:
        hist = lax.all_to_all(hist, "rows", 0, 0, tiled=True)
    return pl.pallas_call(
        gains_kernel,
        out_shape=jax.ShapeDtypeStruct((owned, elect, BINS - 1), jnp.float32),
    )(hist)


def solution(mesh):
    sizes = (mesh.shape["rows"], mesh.shape["feat"])
    return jax.shard_map(
        lambda *arrays: shards(sizes, *arrays),
        mesh=mesh,
        in_specs=(P(("rows", "feat"), None), P("rows"), P("feat", "rows"), P(None, "feat")),
        out_specs=P("rows", "feat", None),
        check_vma=False,
    )
```
